1024 devices in a mesh: group: 64 (over y, z_lo), local: 16 (over z_hi, x, core).
Axes of the slice: x: 4, y: 8, z: 16 (z_hi: 2, z_lo: 8; z = z_hi * 8 + z_lo), core: 2. Of those that a mesh axis runs over, the one named last changes fastest.
Arguments:
- looked_rows: bfloat16 [1024, 4096, 2, 128], P(('group', 'local')), may hold values from -6 to 6
- lengths: int32 [1024, 4096], P(('group', 'local')), may hold values from 0 to 2
- assign: int32 [64, 16], P('group'), may hold values from 0 to 15, each once within a row
- labels: int32 [4096], P('local'), may hold values 0 or 1
- tower_first: bfloat16 [64, 2048, 512], P('group'), may hold values from -0.125 to 0.125
- bias_first: bfloat16 [64, 512], P('group'), may hold values from -3 to 3
- tower_second: bfloat16 [64, 512, 512], P('group'), may hold values from -0.25 to 0.25
- bias_second: bfloat16 [64, 512], P('group'), may hold values from -3 to 3
- over_weight: bfloat16 [32768, 2048], P('group'), may hold values from -0.03125 to 0.03125
- over_bias: bfloat16 [2048], replicated, may hold values from -3 to 3
- out_weight: bfloat16 [2048], replicated, may hold values from -0.125 to 0.125
Outputs:
- scores: float32 [4096], P(('local', 'group'))
- pooled_grad: bfloat16 [1024, 4096, 128], P(('group', 'local'))
The draws below stay inside these ranges and needn't reach their ends.
Inputs may be any that keep to these rules, and one draw needn't show every extreme that they name: Each row of assign names each of 0 to 15 once.
All inputs are finite; a program needn't handle non-finite values. No bound on the sum of `labels` on one device may be relied on, other than what follows from the above.
Results may differ from the reference program's by a relative error of at most 0.014.
Values may be sent and summed in bfloat16 or wider, within the bound.
A program may use at most 32 MiB of HBM per device.

```python
import jax
import jax.numpy as jnp
from jax import lax

E = 128
TW = 512
H = 2048
BAG = 2
TAB_GRP = 16
TABLES = 1024
BATCH = 4096
N_GROUP = 64


def place_ends(entries, own_key, least, largest):
    place = [jax.random.randint(jax.random.fold_in(own_key, axis), (), 0, length) for axis, length in enumerate(entries.shape)]
    main_axis = entries.shape.index(max(entries.shape))
    beside = place[:main_axis] + [(place[main_axis] + 1) % entries.shape[main_axis]] + place[main_axis + 1:]
    return entries.at[tuple(place)].set(least).at[tuple(beside)].set(largest)


def levels(own_key, shape, cuts, least, largest):
    level = 1.0
    for dim, shards_of in cuts:
        heights = jax.random.uniform(jax.random.fold_in(jax.random.fold_in(own_key, 6), dim), (shards_of,), jnp.float32, least / len(cuts), largest / len(cuts))
        level = level * jnp.repeat(jnp.exp(heights), shape[dim] // shards_of).reshape((-1,) + (1,) * (len(shape) - 1 - dim))
    return level


def bell_draw(own_key, extent, scale, most, pieces=(), dtype=jnp.bfloat16):
    level = levels(own_key, extent, pieces, -0.22, 0.18) if pieces else 1.0
    array = jax.random.normal(own_key, extent, jnp.float32) * scale * level
    return jnp.minimum(jnp.maximum(array, -most), most).astype(dtype)


def setup_inputs(seed: int = 0) -> dict:
    keys = jax.random.split(jax.random.key(seed), 12)
    looked_rows = bell_draw(keys[0], (TABLES, BATCH, BAG, E), 1.0, 6.0, ((0, 1024),))
    lengths = place_ends(jax.random.randint(keys[1], (TABLES, BATCH), 0, BAG + 1), jax.random.fold_in(keys[1], 1), 0, BAG).astype(jnp.int32)
    assign = jax.vmap(lambda own: jax.random.permutation(own, TAB_GRP))(jax.random.split(keys[2], N_GROUP)).reshape((N_GROUP, TAB_GRP)).astype(jnp.int32)
    labels = place_ends((jax.random.randint(keys[3], (BATCH,), 0, 2) < 1).astype(jnp.int32), jax.random.fold_in(keys[3], 1), 0, 1)
    tower_first = bell_draw(keys[4], (N_GROUP, TAB_GRP * E, TW), (TAB_GRP * E) ** -0.5, 0.125, ((0, 64),))
    bias_first = bell_draw(keys[5], (N_GROUP, TW), 0.5, 3.0, ((0, 64),))
    tower_second = bell_draw(keys[6], (N_GROUP, TW, TW), TW ** -0.5, 0.25, ((0, 64),))
    bias_second = bell_draw(keys[7], (N_GROUP, TW), 0.5, 3.0, ((0, 64),))
    over_weight = bell_draw(keys[8], (N_GROUP * TW, H), (N_GROUP * TW) ** -0.5, 0.03125, ((0, 64),))
    over_bias = bell_draw(keys[9], (H,), 0.5, 3.0)
    out_weight = bell_draw(keys[10], (H,), H ** -0.5, 0.125)
    return dict(looked_rows=looked_rows, lengths=lengths, assign=assign, labels=labels, tower_first=tower_first, bias_first=bias_first, tower_second=tower_second, bias_second=bias_second, over_weight=over_weight, over_bias=over_bias, out_weight=out_weight)


loss_scale = 2048.0


def silu_slope(values):
    squash = jax.nn.sigmoid(values)
    return squash * (1.0 + values * (1.0 - squash))


def pool_rows(group_rows, group_lengths):
    running = jnp.zeros(group_rows.shape[:2] + group_rows.shape[3:], jnp.float32)
    for position in range(group_rows.shape[2]):
        live_mask = (group_lengths > position)[..., None]
        running = running + jnp.where(live_mask, group_rows[:, :, position, :].astype(jnp.float32), jnp.float32(0.0))
    return running.astype(jnp.bfloat16)


def tower_pass(group_rows, group_lengths, group_assign, first_weight, first_bias, second_weight, second_bias):
    pooled = pool_rows(group_rows, group_lengths)
    slotted = pooled[group_assign]
    tower_in = jnp.transpose(slotted, (1, 0, 2)).reshape(slotted.shape[1], -1)
    first_pre = jnp.dot(tower_in, first_weight, preferred_element_type=jnp.float32) + first_bias.astype(jnp.float32)
    first_act = jax.nn.silu(first_pre).astype(jnp.bfloat16)
    second_pre = jnp.dot(first_act, second_weight, preferred_element_type=jnp.float32) + second_bias.astype(jnp.float32)
    tower_out = jax.nn.silu(second_pre).astype(jnp.bfloat16)
    return first_pre, second_pre, tower_out


def reference(looked_rows, lengths, assign, labels, tower_first, bias_first, tower_second, bias_second, over_weight, over_bias, out_weight):
    group_total = assign.shape[0]
    local_total = assign.shape[1]
    batch_size = lengths.shape[1]
    grouped_rows = looked_rows.reshape((group_total, local_total) + looked_rows.shape[1:])
    grouped_lengths = lengths.reshape(group_total, local_total, batch_size)
    blocks = over_weight.reshape(group_total, -1, over_weight.shape[1])
    tower_inputs = (grouped_rows, grouped_lengths, assign, tower_first, bias_first, tower_second, bias_second, blocks)

    def forward_step(head_total, group_items):
        group_rows, group_lengths, group_assign, first_weight, first_bias, second_weight, second_bias, over_block = group_items
        first_pre, second_pre, tower_out = tower_pass(group_rows, group_lengths, group_assign, first_weight, first_bias, second_weight, second_bias)
        return head_total + jnp.dot(tower_out, over_block, preferred_element_type=jnp.float32), None

    head_start = jnp.zeros((batch_size, over_weight.shape[1]), jnp.float32)
    head_sum, unused = lax.scan(forward_step, head_start, tower_inputs)
    head_pre = head_sum + over_bias.astype(jnp.float32)
    head_out = out_weight.astype(jnp.float32)
    scores = jnp.sum(jax.nn.silu(head_pre) * head_out, axis=1)
    seed_grad = loss_scale * (jax.nn.sigmoid(scores) - labels.astype(jnp.float32))
    head_grad = (seed_grad[:, None] * head_out * silu_slope(head_pre)).astype(jnp.bfloat16)

    def backward_step(group_items):
        group_rows, group_lengths, group_assign, first_weight, first_bias, second_weight, second_bias, over_block = group_items
        first_pre, second_pre, tower_out = tower_pass(group_rows, group_lengths, group_assign, first_weight, first_bias, second_weight, second_bias)
        tower_grad = jnp.dot(head_grad, over_block.T, preferred_element_type=jnp.float32)
        second_grad = (tower_grad * silu_slope(second_pre)).astype(jnp.bfloat16)
        first_grad = (jnp.dot(second_grad, second_weight.T, preferred_element_type=jnp.float32) * silu_slope(first_pre)).astype(jnp.bfloat16)
        input_grad = jnp.dot(first_grad, first_weight.T, preferred_element_type=jnp.float32).astype(jnp.bfloat16)
        slot_grad = jnp.transpose(input_grad.reshape(batch_size, local_total, -1), (1, 0, 2))
        return jnp.zeros_like(slot_grad).at[group_assign].set(slot_grad)

    pooled_grad = lax.map(backward_step, tower_inputs).reshape(looked_rows.shape[0], batch_size, -1)
    return scores, pooled_grad
```

```python
import functools

import jax
import jax.numpy as jnp
from jax import lax
from jax.experimental import pallas as pl
from jax.experimental.pallas import tpu as pltpu
from jax.sharding import PartitionSpec as P

MESH = pl.DeviceIdType.MESH
loss_scale = 2048.0

N = 8
CHUNKS = 4
ROWS = N * N
E = 128
TW = 512
H = 2048
SLOTS = 16
UNIT = 128
LAG = dict(tower=0, gather=2, loss=3, spread=4, back=6, rows=8)


def silu_slope(values):
    squash = jax.nn.sigmoid(values)
    return squash * (1.0 + values * (1.0 - squash))


def silu(values):
    return values * jax.nn.sigmoid(values)


def dot(a, b):
    return jnp.dot(a, b, preferred_element_type=jnp.float32)


def dot_t(a, b):
    return lax.dot_general(a, b, (((1,), (1,)), ((), ())), preferred_element_type=jnp.float32)


def kernel(
    looked_hbm,
    lengths_hbm,
    assign_hbm,
    labels_hbm,
    first_hbm,
    bias_first_hbm,
    second_hbm,
    bias_second_hbm,
    over_hbm,
    over_bias_hbm,
    out_weight_hbm,
    scores_ref,
    grad_hbm,
    assign_ref,
    labels_ref,
    bias_first_ref,
    bias_second_ref,
    over_bias_ref,
    out_weight_ref,
    looked,
    lengths,
    first,
    second,
    over,
    slots,
    pooled,
    arrived,
    part_out,
    part_in,
    first_pre,
    second_pre,
    head_out,
    head_in,
    turn,
    row_out,
    row_in,
    mine_grad,
    line_grad,
    share_grad,
    full_grad,
    own_first_grad,
    far_first_grad,
    table_grad,
    score_out,
    score_in,
    load_sem,
    send_sem,
    arrived_sem,
    part_sem,
    head_sem,
    row_sem,
    line_sem,
    full_sem,
    far_sem,
    grad_sem,
    score_sem,
    score_send_sem,
):
    group = lax.axis_index("group")
    local = lax.axis_index("local")
    y, zl = lax.div(group, N), lax.rem(group, N)
    half, col = lax.div(local, N), lax.rem(local, N)
    other_half = 1 - half

    def turned(at, by):
        return lax.rem(at + by, N)

    def col_peer(d):
        return (group, half * N + turned(col, d))

    def y_peer(d):
        return (turned(y, d) * N + zl, local)

    def z_peer(d):
        return (y * N + turned(zl, d), local)

    far = (group, other_half * N + col)

    def remote(src, dst, ss, rs, to):
        pltpu.make_async_remote_copy(
            src_ref=src, dst_ref=dst, send_sem=ss, recv_sem=rs, device_id=to, device_id_type=MESH
        ).start()

    def wait(ref, sem):
        pltpu.make_async_copy(ref, ref, sem).wait()

    def score_source(i):
        return lax.rem(CHUNKS * group + i, ROWS)

    def score_target(k):
        return lax.div(ROWS * k + group, CHUNKS)

    barrier = pltpu.get_barrier_semaphore()
    for d in range(1, N):
        for peer in (col_peer(d), y_peer(d), z_peer(d)):
            pl.semaphore_signal(barrier, inc=1, device_id=peer, device_id_type=MESH)
    pl.semaphore_signal(barrier, inc=1, device_id=far, device_id_type=MESH)
    for i in range(CHUNKS):

        @pl.when(score_source(i) != group)
        def _():
            pl.semaphore_signal(
                barrier, inc=1, device_id=(score_source(i), local), device_id_type=MESH
            )

    loads = [
        pltpu.make_async_copy(src, dst, load_sem.at[i])
        for i, (src, dst) in enumerate(
            (
                (lengths_hbm, lengths),
                (looked_hbm, looked),
                (assign_hbm, assign_ref),
                (labels_hbm, labels_ref),
                (first_hbm, first),
                (bias_first_hbm, bias_first_ref),
                (second_hbm, second),
                (bias_second_hbm, bias_second_ref),
                (over_hbm, over),
                (over_bias_hbm, over_bias_ref),
                (out_weight_hbm, out_weight_ref),
            )
        )
    ]
    for load in loads:
        load.start()

    def pool_units(parity):
        def pool_unit(block, carry):
            unit = 2 * block + parity
            live = lengths[pl.ds(unit, 1), :]
            row = lax.broadcasted_iota(jnp.int32, (2 * UNIT, UNIT), 0)
            sample = lax.broadcasted_iota(jnp.int32, (2 * UNIT, UNIT), 1)
            place = row - 2 * sample
            mask = jnp.where((place >= 0) & (place < live), 1.0, 0.0).astype(jnp.bfloat16)
            rows = looked[pl.ds(pl.multiple_of(unit * 2 * UNIT, 2 * UNIT), 2 * UNIT), :]
            total = lax.dot_general(
                mask, rows, (((0,), (0,)), ((), ())), preferred_element_type=jnp.float32
            ).astype(jnp.bfloat16)
            for q in range(UNIT // ROWS):
                pooled[lax.rem(block, N), parity * (UNIT // ROWS) + q, lax.div(block, N)] = total[
                    q * ROWS : (q + 1) * ROWS
                ]
            return carry

        lax.fori_loop(0, 2 * N, pool_unit, 0)

    def send_pooled(k):
        for d in range(1, N):
            to = turned(col, d)
            remote(
                pooled.at[to, k],
                arrived.at[k, col],
                send_sem.at[0],
                arrived_sem.at[k],
                (group, half * N + to),
            )
        pltpu.make_async_copy(pooled.at[col, k], arrived.at[k, col], arrived_sem.at[k]).start()

    loads[0].wait()
    loads[1].wait()
    pool_units(0)
    to_come = 3 * (N - 1) + 1
    for k in range(CHUNKS):
        to_come = to_come + jnp.where(score_target(k) != group, 1, 0)
    pl.semaphore_wait(barrier, to_come)
    send_pooled(0)
    send_pooled(1)
    pool_units(1)
    send_pooled(2)
    send_pooled(3)
    for load in loads[2:]:
        load.wait()

    for m in range(N):
        slot = jnp.int32(0)
        for s in range(SLOTS):
            slot = jnp.maximum(slot, jnp.where(assign_ref[0, s] == half * N + m, s, 0))
        slots[m] = slot

    def half_first(k, which):
        total = jnp.zeros((ROWS, TW), jnp.float32)
        for m in range(0, N, 2):
            rows = jnp.concatenate([arrived[k, m, which], arrived[k, m + 1, which]], axis=1)
            weight = jnp.concatenate([first[slots[m]], first[slots[m + 1]]], axis=0)
            total = total + dot(rows, weight)
        return total

    def partial_stage(k):
        wait(arrived.at[k], arrived_sem.at[k])
        part_out[k] = half_first(k, other_half).astype(jnp.bfloat16)
        remote(part_out.at[k], part_in.at[k], send_sem.at[1], part_sem.at[k], far)
        first_pre[k] = half_first(k, half) + bias_first_ref[...].astype(jnp.float32)

    def tower_stage(k):
        wait(part_in.at[k], part_sem.at[k])
        pre = first_pre[k] + part_in[k].astype(jnp.float32)
        first_pre[k] = pre
        act = silu(pre).astype(jnp.bfloat16)
        pre = dot(act, second[...]) + bias_second_ref[...].astype(jnp.float32)
        second_pre[k] = pre
        out = silu(pre).astype(jnp.bfloat16)
        for c in range(2):
            low = dot(out, over[:, c * 512 : (c + 1) * 512])
            high = dot(out, over[:, 1024 + c * 512 : 1024 + (c + 1) * 512])
            for v in range(N):
                head_out[k, v, :, c * 512 : (c + 1) * 512] = jnp.concatenate(
                    [low[v * N : (v + 1) * N], high[v * N : (v + 1) * N]], axis=0
                ).astype(jnp.bfloat16)
        for d in range(1, N):
            to = turned(y, d)
            remote(
                head_out.at[k, to],
                head_in.at[k, y],
                send_sem.at[2],
                head_sem.at[k],
                (to * N + zl, local),
            )
        pltpu.make_async_copy(head_out.at[k, y], head_in.at[k, y], head_sem.at[k]).start()

    def gather_stage(k):
        wait(head_in.at[k], head_sem.at[k])
        total = head_in[k, 0].astype(jnp.float32)
        for v in range(1, N):
            total = total + head_in[k, v].astype(jnp.float32)
        for s in range(2):
            for t in range(N):
                turn[pl.ds((s * N + t) * N, N), :] = total[
                    s * N : (s + 1) * N, t * 128 : (t + 1) * 128
                ]
        for v in range(N):
            row_out[k, v] = jnp.concatenate(
                [turn[pl.ds(s * N * N + v, N, stride=N), :] for s in range(2)], axis=0
            ).astype(jnp.bfloat16)
        for d in range(1, N):
            to = turned(zl, d)
            remote(
                row_out.at[k, to],
                row_in.at[k, zl],
                send_sem.at[3],
                row_sem.at[k],
                (y * N + to, local),
            )
        pltpu.make_async_copy(row_out.at[k, zl], row_in.at[k, zl], row_sem.at[k]).start()

    def loss_stage(k):
        wait(row_in.at[k], row_sem.at[k])
        pre = over_bias_ref[...].astype(jnp.float32)
        for v in range(N):
            pre = pre + row_in[k, v].astype(jnp.float32)
        weight = out_weight_ref[...].astype(jnp.float32)
        score = jnp.sum(
            jnp.sum(silu(pre) * weight, axis=0, keepdims=True), axis=1, keepdims=True
        )
        label = labels_ref[ROWS * k + group].astype(jnp.float32)
        seed = loss_scale * (jax.nn.sigmoid(score) - label)
        mine_grad[k] = (seed * weight * silu_slope(pre)).astype(jnp.bfloat16)
        for d in range(1, N):
            remote(mine_grad.at[k], line_grad.at[k, zl], send_sem.at[4], line_sem.at[k], z_peer(d))
        pltpu.make_async_copy(mine_grad.at[k], line_grad.at[k, zl], line_sem.at[k]).start()
        score_out[k] = jnp.broadcast_to(score, (8, 128))
        target = score_target(k)
        place = lax.rem(group, CHUNKS)

        @pl.when(target != group)
        def _():
            remote(
                score_out.at[k],
                score_in.at[place],
                score_send_sem.at[k],
                score_sem.at[0],
                (target, local),
            )

        @pl.when(target == group)
        def _():
            pltpu.make_async_copy(score_out.at[k], score_in.at[place], score_sem.at[0]).start()

    def spread_stage(k):
        wait(line_grad.at[k], line_sem.at[k])
        for v in range(N):
            turn[pl.ds(v * 2 * N, 2 * N), :] = line_grad[k, v].astype(jnp.float32)
        for t in range(N):
            share_grad[k, :, t * 128 : (t + 1) * 128] = jnp.concatenate(
                [turn[pl.ds(s * N + t, N, stride=2 * N), :] for s in range(2)], axis=0
            ).astype(jnp.bfloat16)
        for d in range(1, N):
            remote(share_grad.at[k], full_grad.at[k, y], send_sem.at[5], full_sem.at[k], y_peer(d))
        pltpu.make_async_copy(share_grad.at[k], full_grad.at[k, y], full_sem.at[k]).start()

    def back_stage(k):
        wait(full_grad.at[k], full_sem.at[k])
        rows = full_grad[k].reshape(2 * ROWS, H // 2)
        low = dot_t(rows, over[:, : H // 2])
        high = dot_t(rows, over[:, H // 2 :])
        tower_grad = jnp.concatenate(
            [
                low[v * 2 * N : v * 2 * N + N] + high[v * 2 * N + N : (v + 1) * 2 * N]
                for v in range(N)
            ],
            axis=0,
        )
        second_grad = (tower_grad * silu_slope(second_pre[k])).astype(jnp.bfloat16)
        own_first_grad[k] = (
            dot_t(second_grad, second[...]) * silu_slope(first_pre[k])
        ).astype(jnp.bfloat16)
        remote(own_first_grad.at[k], far_first_grad.at[k], send_sem.at[6], far_sem.at[k], far)
        half_rows(k, own_first_grad[k], half)

    def half_rows(k, grad, which):
        for m in range(0, N, 2):
            weight = jnp.concatenate([first[slots[m]], first[slots[m + 1]]], axis=0)
            out = dot_t(grad, weight).astype(jnp.bfloat16)
            table_grad[k, m, which] = out[:, :E]
            table_grad[k, m + 1, which] = out[:, E:]

    def rows_stage(k):
        wait(far_first_grad.at[k], far_sem.at[k])
        half_rows(k, far_first_grad[k], other_half)
        span = pl.ds(pl.multiple_of(k * ROWS, ROWS), ROWS)
        for d in range(1, N):
            to = turned(col, d)
            remote(
                table_grad.at[k, to],
                grad_hbm.at[:, col, span],
                send_sem.at[7],
                grad_sem.at[0],
                (group, half * N + to),
            )
        pltpu.make_async_copy(
            table_grad.at[k, col], grad_hbm.at[:, col, span], grad_sem.at[0]
        ).start()

    def partials(k, carry):
        partial_stage(k)
        return carry

    lax.fori_loop(0, CHUNKS, partials, 0)

    stages = (
        (tower_stage, LAG["tower"]),
        (gather_stage, LAG["gather"]),
        (loss_stage, LAG["loss"]),
        (spread_stage, LAG["spread"]),
        (back_stage, LAG["back"]),
        (rows_stage, LAG["rows"]),
    )

    def tick(t, carry):
        for stage, lag in stages:

            @pl.when((t >= lag) & (t < lag + CHUNKS))
            def _():
                stage(t - lag)

        return carry

    lax.fori_loop(0, CHUNKS + LAG["rows"], tick, 0)

    wait(score_in, score_sem.at[0])
    lane = lax.broadcasted_iota(jnp.int32, (8, 128), 1)
    packed = jnp.zeros((8, 128), jnp.float32)
    for i in range(CHUNKS):
        packed = packed + jnp.where(lane == i, score_in[i], 0.0)
    scores_ref[...] = packed

    wait(pooled.at[pl.ds(0, N - 1)], send_sem.at[0])
    wait(part_out, send_sem.at[1])
    wait(head_out.at[:, pl.ds(0, N - 1)], send_sem.at[2])
    wait(row_out.at[:, pl.ds(0, N - 1)], send_sem.at[3])
    wait(line_grad.at[:, pl.ds(0, N - 1)], send_sem.at[4])
    wait(full_grad.at[:, pl.ds(0, N - 1)], send_sem.at[5])
    wait(own_first_grad, send_sem.at[6])
    wait(table_grad.at[:, pl.ds(0, N - 1)], send_sem.at[7])
    for k in range(CHUNKS):

        @pl.when(score_target(k) != group)
        def _():
            wait(score_out.at[k], score_send_sem.at[k])

    wait(table_grad, grad_sem.at[0])


def on_device(
    looked_rows,
    lengths,
    assign,
    labels,
    tower_first,
    bias_first,
    tower_second,
    bias_second,
    over_weight,
    over_bias,
    out_weight,
):
    batch = looked_rows.shape[1]
    block = batch // (2 * N)
    bf16, f32 = jnp.bfloat16, jnp.float32
    any_spec = pl.BlockSpec(memory_space=pl.ANY)
    vmem_spec = pl.BlockSpec(memory_space=pltpu.VMEM)
    dma = pltpu.SemaphoreType.DMA
    scores, grad = pl.pallas_call(
        kernel,
        name="tower_step",
        out_shape=(
            jax.ShapeDtypeStruct((8, 128), f32),
            jax.ShapeDtypeStruct((2, N, block, E), bf16),
        ),
        in_specs=[any_spec] * 11,
        out_specs=(vmem_spec, any_spec),
        scratch_shapes=[
            pltpu.SMEM(assign.shape, jnp.int32),
            pltpu.SMEM(labels.shape, jnp.int32),
            pltpu.VMEM(bias_first.shape, bf16),
            pltpu.VMEM(bias_second.shape, bf16),
            pltpu.VMEM((H // 128, 128), bf16),
            pltpu.VMEM((H // 128, 128), bf16),
            pltpu.VMEM((2 * batch, E), bf16),
            pltpu.VMEM((batch // UNIT, UNIT), jnp.int32),
            pltpu.VMEM((SLOTS, E, TW), bf16),
            pltpu.VMEM((TW, TW), bf16),
            pltpu.VMEM((TW, H), bf16),
            pltpu.SMEM((N,), jnp.int32),
            pltpu.VMEM((N, CHUNKS, 2, ROWS, E), bf16),
            pltpu.VMEM((CHUNKS, N, 2, ROWS, E), bf16),
            pltpu.VMEM((CHUNKS, ROWS, TW), bf16),
            pltpu.VMEM((CHUNKS, ROWS, TW), bf16),
            pltpu.VMEM((CHUNKS, ROWS, TW), f32),
            pltpu.VMEM((CHUNKS, ROWS, TW), f32),
            pltpu.VMEM((CHUNKS, N, 2 * N, H // 2), bf16),
            pltpu.VMEM((CHUNKS, N, 2 * N, H // 2), bf16),
            pltpu.VMEM((2 * N * N, 128), f32),
            pltpu.VMEM((CHUNKS, N, 2 * N, 128), bf16),
            pltpu.VMEM((CHUNKS, N, 2 * N, 128), bf16),
            pltpu.VMEM((CHUNKS, 2 * N, 128), bf16),
            pltpu.VMEM((CHUNKS, N, 2 * N, 128), bf16),
            pltpu.VMEM((CHUNKS, 2 * N, H // 2), bf16),
            pltpu.VMEM((CHUNKS, N, 2 * N, H // 2), bf16),
            pltpu.VMEM((CHUNKS, ROWS, TW), bf16),
            pltpu.VMEM((CHUNKS, ROWS, TW), bf16),
            pltpu.VMEM((CHUNKS, N, 2, ROWS, E), bf16),
            pltpu.VMEM((CHUNKS, 8, 128), f32),
            pltpu.VMEM((CHUNKS, 8, 128), f32),
            dma((11,)),
            dma((8,)),
            dma((CHUNKS,)),
            dma((CHUNKS,)),
            dma((CHUNKS,)),
            dma((CHUNKS,)),
            dma((CHUNKS,)),
            dma((CHUNKS,)),
            dma((CHUNKS,)),
            dma((1,)),
            dma((1,)),
            dma((CHUNKS,)),
        ],
        compiler_params=pltpu.CompilerParams(
            collective_id=0, has_side_effects=True, vmem_limit_bytes=63 * 2**20
        ),
    )(
        looked_rows.reshape(2 * batch, E),
        lengths.reshape(batch // UNIT, UNIT),
        assign,
        labels,
        tower_first.reshape(SLOTS, E, TW),
        bias_first,
        tower_second[0],
        bias_second,
        over_weight,
        over_bias.reshape(H // 128, 128),
        out_weight.reshape(H // 128, 128),
    )
    return scores[0, :CHUNKS], grad.reshape(1, batch, E)


def solution(mesh):
    return jax.shard_map(
        on_device,
        mesh=mesh,
        in_specs=(
            P(("group", "local"), None, None, None),
            P(("group", "local"), None),
            P("group", None),
            P("local"),
            P("group", None, None),
            P("group", None),
            P("group", None, None),
            P("group", None),
            P("group", None),
            P(),
            P(),
        ),
        out_specs=(P(("local", "group")), P(("group", "local"), None, None)),
        check_vma=False,
    )
```

```python
import functools

import jax
import jax.numpy as jnp
from jax import lax
from jax.experimental import pallas as pl
from jax.experimental.pallas import tpu as pltpu
from jax.sharding import PartitionSpec as P

MESH = pl.DeviceIdType.MESH
loss_scale = 2048.0

N = 8
OWN = 4
PAIRS = 4
WIDE = 64
CHUNKS = 2 * PAIRS
ROWS = WIDE // 2
SHARE = ROWS // N
EARLY = 2
QUARTER = 512
E = 128
TW = 512
H = 2048
SLOTS = 16
UNIT = 128
LAST = 20


def silu_slope(values):
    squash = jax.nn.sigmoid(values)
    return squash * (1.0 + values * (1.0 - squash))


def silu(values):
    return values * jax.nn.sigmoid(values)


def dot(a, b):
    return jnp.dot(a, b, preferred_element_type=jnp.float32)


def dot_t(a, b):
    return lax.dot_general(a, b, (((1,), (1,)), ((), ())), preferred_element_type=jnp.float32)


def kernel(
    looked_hbm,
    lengths_hbm,
    assign_hbm,
    labels_hbm,
    first_hbm,
    bias_first_hbm,
    second_hbm,
    bias_second_hbm,
    over_hbm,
    over_bias_hbm,
    out_weight_hbm,
    scores_ref,
    grad_hbm,
    assign_ref,
    labels_ref,
    bias_first_ref,
    bias_second_ref,
    over_bias_ref,
    out_weight_ref,
    looked,
    lengths,
    live,
    first,
    second,
    over,
    slots,
    pooled,
    arrived,
    part_out,
    part_in,
    first_pre,
    second_pre,
    head_out,
    head_in,
    turn,
    bias_turned,
    weight_turned,
    row_out,
    row_in,
    mine_grad,
    line_grad,
    share_grad,
    full_grad,
    own_first_grad,
    far_first_grad,
    table_grad,
    score_out,
    score_in,
    load_sem,
    send_sem,
    arrived_sem,
    part_sem,
    head_sem,
    row_sem,
    line_sem,
    full_sem,
    far_sem,
    grad_sem,
    score_sem,
    score_send_sem,
    part_send_sem,
):
    group = lax.axis_index("group")
    local = lax.axis_index("local")
    y, zl = lax.div(group, N), lax.rem(group, N)
    half, col = lax.div(local, N), lax.rem(local, N)
    other_half = 1 - half

    def turned(at, by):
        return lax.rem(at + by, N)

    def col_peer(d):
        return (group, half * N + turned(col, d))

    def y_peer(d):
        return (turned(y, d) * N + zl, local)

    def z_peer(d):
        return (y * N + turned(zl, d), local)

    far = (group, other_half * N + col)

    def remote(src, dst, ss, rs, to):
        pltpu.make_async_remote_copy(
            src_ref=src, dst_ref=dst, send_sem=ss, recv_sem=rs, device_id=to, device_id_type=MESH
        ).start()

    def wait(ref, sem):
        pltpu.make_async_copy(ref, ref, sem).wait()

    side, lane_row = lax.div(zl, SHARE), lax.rem(zl, SHARE)

    def score_source(i):
        return zl * N + SHARE * lax.rem(y, 2) + i

    def score_target(e):
        return (2 * e + side) * N + y

    barrier = pltpu.get_barrier_semaphore()
    for d in range(1, N):
        for peer in (col_peer(d), y_peer(d), z_peer(d)):
            pl.semaphore_signal(barrier, inc=1, device_id=peer, device_id_type=MESH)
    pl.semaphore_signal(barrier, inc=1, device_id=far, device_id_type=MESH)
    for i in range(OWN):

        @pl.when(score_source(i) != group)
        def _():
            pl.semaphore_signal(
                barrier, inc=1, device_id=(score_source(i), local), device_id_type=MESH
            )

    loads = [
        pltpu.make_async_copy(src, dst, load_sem.at[i])
        for i, (src, dst) in enumerate(
            (
                (lengths_hbm, lengths),
                (looked_hbm, looked),
                (assign_hbm, assign_ref),
                (labels_hbm, labels_ref),
                (first_hbm, first),
                (bias_first_hbm, bias_first_ref),
                (second_hbm, second),
                (bias_second_hbm, bias_second_ref),
                (over_hbm, over),
                (over_bias_hbm, over_bias_ref),
                (out_weight_hbm, out_weight_ref),
            )
        )
    ]
    for load in loads:
        load.start()

    def pool_units(parity):
        def pool_unit(block, carry):
            unit = 2 * block + parity
            rows = looked[pl.ds(pl.multiple_of(unit * 2 * UNIT, 2 * UNIT), 2 * UNIT), :]
            mask = jnp.where(pair, live[pl.ds(unit, 1), :], 0.0).astype(jnp.bfloat16)
            total = dot(mask, rows).astype(jnp.bfloat16)
            for q in range(UNIT // WIDE):
                pooled[lax.rem(block, N), parity * (UNIT // WIDE) + q, lax.div(block, N)] = total[
                    q * WIDE : (q + 1) * WIDE
                ]
            return carry

        lax.fori_loop(0, 2 * N, pool_unit, 0, unroll=8)

    def send_pooled(k):
        for d in range(1, N):
            to = turned(col, d)
            remote(
                pooled.at[to, k],
                arrived.at[k, col],
                send_sem.at[0],
                arrived_sem.at[k],
                (group, half * N + to),
            )
        pltpu.make_async_copy(pooled.at[col, k], arrived.at[k, col], arrived_sem.at[k]).start()

    loads[0].wait()
    row = lax.broadcasted_iota(jnp.int32, (UNIT, 2 * UNIT), 1)
    place = row - 2 * lax.broadcasted_iota(jnp.int32, (UNIT, 2 * UNIT), 0)
    pair = (place >= 0) & (place < 2)
    twice = dot(
        lengths[...].astype(jnp.float32).astype(jnp.bfloat16),
        jnp.where(pair, 1.0, 0.0).astype(jnp.bfloat16),
    )
    position = lax.rem(lax.broadcasted_iota(jnp.int32, twice.shape, 1), 2).astype(jnp.float32)
    live[...] = jnp.where(twice > position, 1.0, 0.0)
    loads[1].wait()
    pool_units(0)
    to_come = 3 * (N - 1) + 1
    for e in range(OWN):
        to_come = to_come + jnp.where(score_target(e) != group, 1, 0)
    pl.semaphore_wait(barrier, to_come)
    send_pooled(0)
    pool_units(1)
    send_pooled(1)
    for load in loads[2:]:
        load.wait()

    for m in range(N):
        slot = jnp.int32(0)
        for s in range(SLOTS):
            slot = jnp.maximum(slot, jnp.where(assign_ref[0, s] == half * N + m, s, 0))
        slots[m] = slot

    turn[pl.ds(0, 16), :] = over_bias_ref[...].astype(jnp.float32)
    turn[pl.ds(16, 16), :] = out_weight_ref[...].astype(jnp.float32)
    for t in range(4):
        bias_turned[t * 4 : (t + 1) * 4, :] = turn[pl.ds(t, 4, stride=4), :]
        weight_turned[t * 4 : (t + 1) * 4, :] = turn[pl.ds(16 + t, 4, stride=4), :]

    def partial_stage(p):
        wait(arrived.at[p], arrived_sem.at[p])

        @pl.when(p + 2 < PAIRS)
        def _():
            send_pooled(p + 2)

        total = jnp.zeros((2 * WIDE, TW), jnp.float32)
        for m in range(0, N, 2):
            rows = jnp.concatenate(
                [
                    jnp.concatenate([arrived[p, m, which], arrived[p, m + 1, which]], axis=1)
                    for which in (other_half, half)
                ],
                axis=0,
            )
            weight = jnp.concatenate([first[slots[m]], first[slots[m + 1]]], axis=0)
            total = total + dot(rows, weight)
        bias = bias_first_ref[...].astype(jnp.float32)
        for q in range(2):
            k = 2 * p + q
            part_out[k] = total[q * ROWS : (q + 1) * ROWS].astype(jnp.bfloat16)
            first_pre[k] = total[WIDE + q * ROWS : WIDE + (q + 1) * ROWS] + bias

        @pl.when(p > 0)
        def _():
            wait(part_out.at[pl.ds(2 * p - 2, 2)], part_send_sem.at[p - 1])

        for q in range(2):
            k = 2 * p + q
            remote(part_out.at[k], part_in.at[k], part_send_sem.at[p], part_sem.at[k], far)

    def tower_stage(k):
        wait(part_in.at[k], part_sem.at[k])
        pre = first_pre[k] + part_in[k].astype(jnp.float32)
        first_pre[k] = pre
        act = silu(pre).astype(jnp.bfloat16)
        pre = dot(act, second[...]) + bias_second_ref[...].astype(jnp.float32)
        second_pre[k] = pre
        out = silu(pre).astype(jnp.bfloat16)
        parts = [dot(out, over[:, q * QUARTER : (q + 1) * QUARTER]) for q in range(4)]
        for v in range(N):
            head_out[k, v] = jnp.concatenate(
                [part[v * SHARE : (v + 1) * SHARE] for part in parts], axis=0
            ).astype(jnp.bfloat16)
        for d in range(1, N):
            to = turned(y, d)
            remote(
                head_out.at[k, to],
                head_in.at[k, y],
                send_sem.at[2],
                head_sem.at[k],
                (to * N + zl, local),
            )
        pltpu.make_async_copy(head_out.at[k, y], head_in.at[k, y], head_sem.at[k]).start()

    def gather_stage(k):
        wait(head_in.at[k], head_sem.at[k])
        total = head_in[k, 0].astype(jnp.float32)
        for v in range(1, N):
            total = total + head_in[k, v].astype(jnp.float32)
        for t in range(4):
            turn[t * 16 : (t + 1) * 16, :] = total[:, t * 128 : (t + 1) * 128]
        for r in range(SHARE):
            row_out[k, r] = turn[pl.ds(r, 16, stride=SHARE), :].astype(jnp.bfloat16)
        e = lax.div(k, 2)
        for r in range(SHARE):
            to = SHARE * lax.rem(k, 2) + r

            @pl.when(to != zl)
            def _():
                remote(
                    row_out.at[k, r],
                    row_in.at[e, zl],
                    send_sem.at[3],
                    row_sem.at[e],
                    (y * N + to, local),
                )

            @pl.when(to == zl)
            def _():
                pltpu.make_async_copy(row_out.at[k, r], row_in.at[e, zl], row_sem.at[e]).start()

    def loss_stage(k):
        @pl.when(lax.rem(k, 2) == side)
        def _():
            loss_row(k, lax.div(k, 2))

    def loss_row(k, e):
        wait(row_in.at[e], row_sem.at[e])
        pre = bias_turned[...]
        for v in range(N):
            pre = pre + row_in[e, v].astype(jnp.float32)
        weight = weight_turned[...]
        score = jnp.sum(
            jnp.sum(silu(pre) * weight, axis=0, keepdims=True), axis=1, keepdims=True
        )
        label = labels_ref[ROWS * k + SHARE * y + lane_row].astype(jnp.float32)
        seed = loss_scale * (jax.nn.sigmoid(score) - label)
        mine_grad[e] = (seed * weight * silu_slope(pre)).astype(jnp.bfloat16)
        for d in range(1, N):
            remote(
                mine_grad.at[e],
                line_grad.at[k, lane_row],
                send_sem.at[4],
                line_sem.at[k],
                z_peer(d),
            )
        pltpu.make_async_copy(mine_grad.at[e], line_grad.at[k, lane_row], line_sem.at[k]).start()
        score_out[e] = jnp.broadcast_to(score, (8, 128))
        target = score_target(e)

        @pl.when(target != group)
        def _():
            remote(
                score_out.at[e],
                score_in.at[lane_row],
                score_send_sem.at[e],
                score_sem.at[0],
                (target, local),
            )

        @pl.when(target == group)
        def _():
            pltpu.make_async_copy(score_out.at[e], score_in.at[lane_row], score_sem.at[0]).start()

    def spread_stage(k):
        wait(line_grad.at[k], line_sem.at[k])
        for r in range(SHARE):
            turn[r * 16 : (r + 1) * 16, :] = line_grad[k, r].astype(jnp.float32)
        for t in range(4):
            share_grad[k, :, t * 128 : (t + 1) * 128] = jnp.concatenate(
                [turn[pl.ds(t * 4 + q, SHARE, stride=16), :] for q in range(4)], axis=0
            ).astype(jnp.bfloat16)
        for d in range(1, N):
            remote(share_grad.at[k], full_grad.at[k, y], send_sem.at[5], full_sem.at[k], y_peer(d))
        pltpu.make_async_copy(share_grad.at[k], full_grad.at[k, y], full_sem.at[k]).start()

    def back_stage(k):
        wait(full_grad.at[k], full_sem.at[k])
        rows = full_grad[k].reshape(N * 16, QUARTER)
        parts = [dot_t(rows, over[:, q * QUARTER : (q + 1) * QUARTER]) for q in range(4)]
        low = lax.rem(lax.broadcasted_iota(jnp.int32, (8, TW), 0), 8) < SHARE
        sums = []
        for v in range(N):
            both = jnp.where(
                low, parts[0][v * 16 : v * 16 + 8], parts[1][v * 16 : v * 16 + 8]
            ) + jnp.where(
                low, parts[2][v * 16 + 8 : v * 16 + 16], parts[3][v * 16 + 8 : v * 16 + 16]
            )
            sums.append(both[:SHARE] + both[SHARE:])
        tower_grad = jnp.concatenate(sums, axis=0)
        second_grad = (tower_grad * silu_slope(second_pre[k])).astype(jnp.bfloat16)
        own_first_grad[k] = (
            dot_t(second_grad, second[...]) * silu_slope(first_pre[k])
        ).astype(jnp.bfloat16)
        remote(own_first_grad.at[k], far_first_grad.at[k], send_sem.at[6], far_sem.at[k], far)

    def rows_stage(p):
        pair = pl.ds(2 * p, 2)
        for q in range(2):
            wait(far_first_grad.at[2 * p + q], far_sem.at[2 * p + q])
        grad = jnp.concatenate(
            [
                own_first_grad[pair].reshape(WIDE, TW),
                far_first_grad[pair].reshape(WIDE, TW),
            ],
            axis=0,
        )
        for m in range(0, N, 2):
            weight = jnp.concatenate([first[slots[m]], first[slots[m + 1]]], axis=0)
            out = dot_t(grad, weight).astype(jnp.bfloat16)
            for v in range(2):
                table_grad[p, m + v, half] = out[:WIDE, v * E : (v + 1) * E]
                table_grad[p, m + v, other_half] = out[WIDE:, v * E : (v + 1) * E]
        span = pl.ds(pl.multiple_of(p * WIDE, WIDE), WIDE)
        for d in range(1, N):
            to = turned(col, d)
            remote(
                table_grad.at[p, to],
                grad_hbm.at[:, col, span],
                send_sem.at[7],
                grad_sem.at[0],
                (group, half * N + to),
            )
        pltpu.make_async_copy(
            table_grad.at[p, col], grad_hbm.at[:, col, span], grad_sem.at[0]
        ).start()

    def partials(p, carry):
        partial_stage(p)
        return carry

    lax.fori_loop(0, EARLY, partials, 0)

    stages = (
        (tower_stage, 0),
        (gather_stage, 4),
        (loss_stage, 8),
        (spread_stage, 12),
        (back_stage, 16),
    )

    def tick(t, carry):
        for stage, lag in stages:

            @pl.when((t >= lag) & (t < lag + CHUNKS))
            def _():
                stage(t - lag)

            if lag == 0:

                @pl.when((t < 2 * (PAIRS - EARLY)) & (lax.rem(t, 2) == 0))
                def _():
                    partial_stage(EARLY + lax.div(t, 2))

        @pl.when((t >= LAST) & (lax.rem(t - LAST, 2) == 0))
        def _():
            rows_stage(lax.div(t - LAST, 2))

        return carry

    lax.fori_loop(0, LAST + CHUNKS - 1, tick, 0)

    wait(score_in, score_sem.at[0])
    lane = lax.broadcasted_iota(jnp.int32, (8, 128), 1)
    packed = jnp.zeros((8, 128), jnp.float32)
    for i in range(OWN):
        packed = packed + jnp.where(lane == i, score_in[i], 0.0)
    scores_ref[...] = packed

    wait(pooled.at[pl.ds(0, N - 1)], send_sem.at[0])
    wait(part_out.at[pl.ds(CHUNKS - 2, 2)], part_send_sem.at[PAIRS - 1])
    wait(head_out.at[:, pl.ds(0, N - 1)], send_sem.at[2])
    wait(row_out.at[pl.ds(0, CHUNKS - 1)], send_sem.at[3])
    wait(line_grad.at[pl.ds(0, CHUNKS - 1)], send_sem.at[4])
    wait(full_grad.at[:, pl.ds(0, N - 1)], send_sem.at[5])
    wait(own_first_grad, send_sem.at[6])
    wait(table_grad.at[:, pl.ds(0, N - 1)], send_sem.at[7])
    for e in range(OWN):

        @pl.when(score_target(e) != group)
        def _():
            wait(score_out.at[e], score_send_sem.at[e])

    wait(table_grad, grad_sem.at[0])


def on_device(
    looked_rows,
    lengths,
    assign,
    labels,
    tower_first,
    bias_first,
    tower_second,
    bias_second,
    over_weight,
    over_bias,
    out_weight,
):
    batch = looked_rows.shape[1]
    block = batch // (2 * N)
    bf16, f32 = jnp.bfloat16, jnp.float32
    any_spec = pl.BlockSpec(memory_space=pl.ANY)
    vmem_spec = pl.BlockSpec(memory_space=pltpu.VMEM)
    dma = pltpu.SemaphoreType.DMA
    scores, grad = pl.pallas_call(
        kernel,
        name="tower_step",
        out_shape=(
            jax.ShapeDtypeStruct((8, 128), f32),
            jax.ShapeDtypeStruct((2, N, block, E), bf16),
        ),
        in_specs=[any_spec] * 11,
        out_specs=(vmem_spec, any_spec),
        scratch_shapes=[
            pltpu.SMEM(assign.shape, jnp.int32),
            pltpu.SMEM(labels.shape, jnp.int32),
            pltpu.VMEM(bias_first.shape, bf16),
            pltpu.VMEM(bias_second.shape, bf16),
            pltpu.VMEM((H // 128, 128), bf16),
            pltpu.VMEM((H // 128, 128), bf16),
            pltpu.VMEM((2 * batch, E), bf16),
            pltpu.VMEM((batch // UNIT, UNIT), jnp.int32),
            pltpu.VMEM((batch // UNIT, 2 * UNIT), f32),
            pltpu.VMEM((SLOTS, E, TW), bf16),
            pltpu.VMEM((TW, TW), bf16),
            pltpu.VMEM((TW, H), bf16),
            pltpu.SMEM((N,), jnp.int32),
            pltpu.VMEM((N, PAIRS, 2, WIDE, E), bf16),
            pltpu.VMEM((PAIRS, N, 2, WIDE, E), bf16),
            pltpu.VMEM((CHUNKS, ROWS, TW), bf16),
            pltpu.VMEM((CHUNKS, ROWS, TW), bf16),
            pltpu.VMEM((CHUNKS, ROWS, TW), f32),
            pltpu.VMEM((CHUNKS, ROWS, TW), f32),
            pltpu.VMEM((CHUNKS, N, 16, QUARTER), bf16),
            pltpu.VMEM((CHUNKS, N, 16, QUARTER), bf16),
            pltpu.VMEM((64, 128), f32),
            pltpu.VMEM((16, 128), f32),
            pltpu.VMEM((16, 128), f32),
            pltpu.VMEM((CHUNKS, SHARE, 16, 128), bf16),
            pltpu.VMEM((CHUNKS // 2, N, 16, 128), bf16),
            pltpu.VMEM((CHUNKS // 2, 16, 128), bf16),
            pltpu.VMEM((CHUNKS, SHARE, 16, 128), bf16),
            pltpu.VMEM((CHUNKS, 16, QUARTER), bf16),
            pltpu.VMEM((CHUNKS, N, 16, QUARTER), bf16),
            pltpu.VMEM((CHUNKS, ROWS, TW), bf16),
            pltpu.VMEM((CHUNKS, ROWS, TW), bf16),
            pltpu.VMEM((PAIRS, N, 2, WIDE, E), bf16),
            pltpu.VMEM((OWN, 8, 128), f32),
            pltpu.VMEM((OWN, 8, 128), f32),
            dma((11,)),
            dma((8,)),
            dma((PAIRS,)),
            dma((CHUNKS,)),
            dma((CHUNKS,)),
            dma((CHUNKS // 2,)),
            dma((CHUNKS,)),
            dma((CHUNKS,)),
            dma((CHUNKS,)),
            dma((1,)),
            dma((1,)),
            dma((OWN,)),
            dma((PAIRS,)),
        ],
        compiler_params=pltpu.CompilerParams(
            collective_id=0, has_side_effects=True, vmem_limit_bytes=63 * 2**20
        ),
    )(
        looked_rows.reshape(2 * batch, E),
        lengths.reshape(batch // UNIT, UNIT),
        assign,
        labels,
        tower_first.reshape(SLOTS, E, TW),
        bias_first,
        tower_second[0],
        bias_second,
        over_weight,
        over_bias.reshape(H // 128, 128),
        out_weight.reshape(H // 128, 128),
    )
    return scores[0, :OWN], grad.reshape(1, batch, E)


def solution(mesh):
    return jax.shard_map(
        on_device,
        mesh=mesh,
        in_specs=(
            P(("group", "local"), None, None, None),
            P(("group", "local"), None),
            P("group", None),
            P("local"),
            P("group", None, None),
            P("group", None),
            P("group", None, None),
            P("group", None),
            P("group", None),
            P(),
            P(),
        ),
        out_specs=(P(("local", "group")), P(("group", "local"), None, None)),
        check_vma=False,
    )
```

```python
import functools

import jax
import jax.numpy as jnp
from jax import lax
from jax.experimental import pallas as pl
from jax.experimental.pallas import tpu as pltpu
from jax.sharding import PartitionSpec as P

MESH = pl.DeviceIdType.MESH
loss_scale = 2048.0

N = 8
OWN = 4
PAIRS = 4
WIDE = 64
CHUNKS = 2 * PAIRS
ROWS = WIDE // 2
SHARE = ROWS // N
EARLY = 2
QUARTER = 512
E = 128
TW = 512
H = 2048
SLOTS = 16
UNIT = 128
LAST = 20


def silu_slope(values):
    squash = jax.nn.sigmoid(values)
    return squash * (1.0 + values * (1.0 - squash))


def silu(values):
    return values * jax.nn.sigmoid(values)


def dot(a, b):
    return jnp.dot(a, b, preferred_element_type=jnp.float32)


def dot_t(a, b):
    return lax.dot_general(a, b, (((1,), (1,)), ((), ())), preferred_element_type=jnp.float32)


def kernel(
    looked_hbm,
    lengths_hbm,
    assign_hbm,
    labels_hbm,
    first_hbm,
    bias_first_hbm,
    second_hbm,
    bias_second_hbm,
    over_hbm,
    over_bias_hbm,
    out_weight_hbm,
    scores_ref,
    grad_hbm,
    assign_ref,
    labels_ref,
    bias_first_ref,
    bias_second_ref,
    over_bias_ref,
    out_weight_ref,
    looked,
    lengths,
    live,
    first,
    second,
    over,
    slots,
    pooled,
    arrived,
    part_out,
    part_in,
    first_pre,
    second_pre,
    head_out,
    head_in,
    turn,
    bias_turned,
    weight_turned,
    row_out,
    row_in,
    mine_grad,
    line_grad,
    share_grad,
    full_grad,
    own_first_grad,
    far_first_grad,
    table_grad,
    score_out,
    score_in,
    load_sem,
    send_sem,
    arrived_sem,
    part_sem,
    head_sem,
    row_sem,
    line_sem,
    full_sem,
    far_sem,
    grad_sem,
    score_sem,
    score_send_sem,
    part_send_sem,
):
    group = lax.axis_index("group")
    local = lax.axis_index("local")
    y, zl = lax.div(group, N), lax.rem(group, N)
    half, col = lax.div(local, N), lax.rem(local, N)
    other_half = 1 - half

    def turned(at, by):
        return lax.rem(at + by, N)

    def col_peer(d):
        return (group, half * N + turned(col, d))

    def y_peer(d):
        return (turned(y, d) * N + zl, local)

    def z_peer(d):
        return (y * N + turned(zl, d), local)

    far = (group, other_half * N + col)

    def remote(src, dst, ss, rs, to):
        pltpu.make_async_remote_copy(
            src_ref=src, dst_ref=dst, send_sem=ss, recv_sem=rs, device_id=to, device_id_type=MESH
        ).start()

    def wait(ref, sem):
        pltpu.make_async_copy(ref, ref, sem).wait()

    side, lane_row = lax.div(zl, SHARE), lax.rem(zl, SHARE)

    def score_source(i):
        return zl * N + SHARE * lax.rem(y, 2) + i

    def score_target(e):
        return (2 * e + side) * N + y

    barrier = pltpu.get_barrier_semaphore()
    for d in range(1, N):
        for peer in (col_peer(d), y_peer(d), z_peer(d)):
            pl.semaphore_signal(barrier, inc=1, device_id=peer, device_id_type=MESH)
    pl.semaphore_signal(barrier, inc=1, device_id=far, device_id_type=MESH)
    for i in range(OWN):

        @pl.when(score_source(i) != group)
        def _():
            pl.semaphore_signal(
                barrier, inc=1, device_id=(score_source(i), local), device_id_type=MESH
            )

    loads = [
        pltpu.make_async_copy(src, dst, load_sem.at[i])
        for i, (src, dst) in enumerate(
            (
                (lengths_hbm, lengths),
                (looked_hbm, looked),
                (assign_hbm, assign_ref),
                (labels_hbm, labels_ref),
                (first_hbm, first),
                (bias_first_hbm, bias_first_ref),
                (second_hbm, second),
                (bias_second_hbm, bias_second_ref),
                (over_hbm, over),
                (over_bias_hbm, over_bias_ref),
                (out_weight_hbm, out_weight_ref),
            )
        )
    ]
    for load in loads:
        load.start()

    def pool_units(parity):
        def pool_unit(block, carry):
            unit = 2 * block + parity
            rows = looked[pl.ds(pl.multiple_of(unit * 2 * UNIT, 2 * UNIT), 2 * UNIT), :]
            mask = jnp.where(pair, live[pl.ds(unit, 1), :], 0.0).astype(jnp.bfloat16)
            total = dot(mask, rows).astype(jnp.bfloat16)
            for q in range(UNIT // WIDE):
                pooled[lax.rem(block, N), parity * (UNIT // WIDE) + q, lax.div(block, N)] = total[
                    q * WIDE : (q + 1) * WIDE
                ]
            return carry

        lax.fori_loop(0, 2 * N, pool_unit, 0, unroll=8)

    def send_pooled(k):
        for d in range(1, N):
            to = turned(col, d)
            remote(
                pooled.at[to, k],
                arrived.at[k, col],
                send_sem.at[0],
                arrived_sem.at[k],
                (group, half * N + to),
            )
        pltpu.make_async_copy(pooled.at[col, k], arrived.at[k, col], arrived_sem.at[k]).start()

    loads[0].wait()
    row = lax.broadcasted_iota(jnp.int32, (UNIT, 2 * UNIT), 1)
    place = row - 2 * lax.broadcasted_iota(jnp.int32, (UNIT, 2 * UNIT), 0)
    pair = (place >= 0) & (place < 2)
    twice = dot(
        lengths[...].astype(jnp.float32).astype(jnp.bfloat16),
        jnp.where(pair, 1.0, 0.0).astype(jnp.bfloat16),
    )
    position = lax.rem(lax.broadcasted_iota(jnp.int32, twice.shape, 1), 2).astype(jnp.float32)
    live[...] = jnp.where(twice > position, 1.0, 0.0)
    loads[1].wait()
    pool_units(0)
    to_come = 3 * (N - 1) + 1
    for e in range(OWN):
        to_come = to_come + jnp.where(score_target(e) != group, 1, 0)
    pl.semaphore_wait(barrier, to_come)
    send_pooled(0)
    pool_units(1)
    send_pooled(1)
    for load in loads[2:]:
        load.wait()

    for m in range(N):
        slot = jnp.int32(0)
        for s in range(SLOTS):
            slot = jnp.maximum(slot, jnp.where(assign_ref[0, s] == half * N + m, s, 0))
        slots[m] = slot

    turn[pl.ds(0, 16), :] = over_bias_ref[...].astype(jnp.float32)
    turn[pl.ds(16, 16), :] = out_weight_ref[...].astype(jnp.float32)
    for t in range(4):
        bias_turned[t * 4 : (t + 1) * 4, :] = turn[pl.ds(t, 4, stride=4), :]
        weight_turned[t * 4 : (t + 1) * 4, :] = turn[pl.ds(16 + t, 4, stride=4), :]

    def partial_stage(p):
        wait(arrived.at[p], arrived_sem.at[p])

        @pl.when(p + 2 < PAIRS)
        def _():
            send_pooled(p + 2)

        total = jnp.zeros((2 * WIDE, TW), jnp.float32)
        for m in range(0, N, 2):
            rows = jnp.concatenate(
                [
                    jnp.concatenate([arrived[p, m, which], arrived[p, m + 1, which]], axis=1)
                    for which in (other_half, half)
                ],
                axis=0,
            )
            weight = jnp.concatenate([first[slots[m]], first[slots[m + 1]]], axis=0)
            total = total + dot(rows, weight)
        bias = bias_first_ref[...].astype(jnp.float32)
        for q in range(2):
            k = 2 * p + q
            part_out[k] = total[q * ROWS : (q + 1) * ROWS].astype(jnp.bfloat16)
            first_pre[k] = total[WIDE + q * ROWS : WIDE + (q + 1) * ROWS] + bias

        @pl.when(p > 0)
        def _():
            wait(part_out.at[pl.ds(2 * p - 2, 2)], part_send_sem.at[p - 1])

        for q in range(2):
            k = 2 * p + q
            remote(part_out.at[k], part_in.at[k], part_send_sem.at[p], part_sem.at[k], far)

    def tower_stage(k):
        wait(part_in.at[k], part_sem.at[k])
        pre = first_pre[k] + part_in[k].astype(jnp.float32)
        first_pre[k] = pre
        act = silu(pre).astype(jnp.bfloat16)
        pre = dot(act, second[...]) + bias_second_ref[...].astype(jnp.float32)
        second_pre[k] = pre
        out = silu(pre).astype(jnp.bfloat16)
        parts = [dot(out, over[:, q * QUARTER : (q + 1) * QUARTER]) for q in range(4)]
        for v in range(N):
            head_out[k, v] = jnp.concatenate(
                [part[v * SHARE : (v + 1) * SHARE] for part in parts], axis=0
            ).astype(jnp.bfloat16)
        for d in range(1, N):
            to = turned(y, d)
            remote(
                head_out.at[k, to],
                head_in.at[k, y],
                send_sem.at[2],
                head_sem.at[k],
                (to * N + zl, local),
            )
        pltpu.make_async_copy(head_out.at[k, y], head_in.at[k, y], head_sem.at[k]).start()

    def gather_stage(k):
        wait(head_in.at[k], head_sem.at[k])
        total = head_in[k, 0].astype(jnp.float32)
        for v in range(1, N):
            total = total + head_in[k, v].astype(jnp.float32)
        for t in range(4):
            turn[t * 16 : (t + 1) * 16, :] = total[:, t * 128 : (t + 1) * 128]
        for r in range(SHARE):
            row_out[k, r] = turn[pl.ds(r, 16, stride=SHARE), :].astype(jnp.bfloat16)
        e = lax.div(k, 2)
        for r in range(SHARE):
            to = SHARE * lax.rem(k, 2) + r

            @pl.when(to != zl)
            def _():
                remote(
                    row_out.at[k, r],
                    row_in.at[e, zl],
                    send_sem.at[3],
                    row_sem.at[e],
                    (y * N + to, local),
                )

            @pl.when(to == zl)
            def _():
                pltpu.make_async_copy(row_out.at[k, r], row_in.at[e, zl], row_sem.at[e]).start()

    def loss_stage(k):
        @pl.when(lax.rem(k, 2) == side)
        def _():
            loss_row(k, lax.div(k, 2))

    def loss_row(k, e):
        wait(row_in.at[e], row_sem.at[e])
        pre = bias_turned[...]
        for v in range(N):
            pre = pre + row_in[e, v].astype(jnp.float32)
        weight = weight_turned[...]
        score = jnp.sum(
            jnp.sum(silu(pre) * weight, axis=0, keepdims=True), axis=1, keepdims=True
        )
        label = labels_ref[ROWS * k + SHARE * y + lane_row].astype(jnp.float32)
        seed = loss_scale * (jax.nn.sigmoid(score) - label)
        mine_grad[e] = (seed * weight * silu_slope(pre)).astype(jnp.bfloat16)
        for d in range(1, N):
            remote(
                mine_grad.at[e],
                line_grad.at[k, lane_row],
                send_sem.at[4],
                line_sem.at[k],
                z_peer(d),
            )
        pltpu.make_async_copy(mine_grad.at[e], line_grad.at[k, lane_row], line_sem.at[k]).start()
        score_out[e] = jnp.broadcast_to(score, (8, 128))
        target = score_target(e)

        @pl.when(target != group)
        def _():
            remote(
                score_out.at[e],
                score_in.at[lane_row],
                score_send_sem.at[e],
                score_sem.at[0],
                (target, local),
            )

        @pl.when(target == group)
        def _():
            pltpu.make_async_copy(score_out.at[e], score_in.at[lane_row], score_sem.at[0]).start()

    def spread_stage(k):
        wait(line_grad.at[k], line_sem.at[k])
        for r in range(SHARE):
            turn[r * 16 : (r + 1) * 16, :] = line_grad[k, r].astype(jnp.float32)
        for t in range(4):
            share_grad[k, :, t * 128 : (t + 1) * 128] = jnp.concatenate(
                [turn[pl.ds(t * 4 + q, SHARE, stride=16), :] for q in range(4)], axis=0
            ).astype(jnp.bfloat16)
        for d in range(1, N):
            remote(share_grad.at[k], full_grad.at[k, y], send_sem.at[5], full_sem.at[k], y_peer(d))
        pltpu.make_async_copy(share_grad.at[k], full_grad.at[k, y], full_sem.at[k]).start()

    def back_stage(k):
        wait(full_grad.at[k], full_sem.at[k])
        rows = full_grad[k].reshape(N * 16, QUARTER)
        parts = [dot_t(rows, over[:, q * QUARTER : (q + 1) * QUARTER]) for q in range(4)]
        low = lax.rem(lax.broadcasted_iota(jnp.int32, (8, TW), 0), 8) < SHARE
        sums = []
        for v in range(N):
            both = jnp.where(
                low, parts[0][v * 16 : v * 16 + 8], parts[1][v * 16 : v * 16 + 8]
            ) + jnp.where(
                low, parts[2][v * 16 + 8 : v * 16 + 16], parts[3][v * 16 + 8 : v * 16 + 16]
            )
            sums.append(both[:SHARE] + both[SHARE:])
        tower_grad = jnp.concatenate(sums, axis=0)
        second_grad = (tower_grad * silu_slope(second_pre[k])).astype(jnp.bfloat16)
        own_first_grad[k] = (
            dot_t(second_grad, second[...]) * silu_slope(first_pre[k])
        ).astype(jnp.bfloat16)
        remote(own_first_grad.at[k], far_first_grad.at[k], send_sem.at[6], far_sem.at[k], far)

    def rows_stage(k):
        wait(far_first_grad.at[k], far_sem.at[k])
        grad = jnp.concatenate([own_first_grad[k], far_first_grad[k]], axis=0)
        for m in range(0, N, 2):
            weight = jnp.concatenate([first[slots[m]], first[slots[m + 1]]], axis=0)
            out = dot_t(grad, weight).astype(jnp.bfloat16)
            for v in range(2):
                table_grad[k, m + v, half] = out[:ROWS, v * E : (v + 1) * E]
                table_grad[k, m + v, other_half] = out[ROWS:, v * E : (v + 1) * E]
        span = pl.ds(pl.multiple_of(k * ROWS, ROWS), ROWS)
        for d in range(1, N):
            to = turned(col, d)
            remote(
                table_grad.at[k, to],
                grad_hbm.at[:, col, span],
                send_sem.at[7],
                grad_sem.at[0],
                (group, half * N + to),
            )
        pltpu.make_async_copy(
            table_grad.at[k, col], grad_hbm.at[:, col, span], grad_sem.at[0]
        ).start()

    def partials(p, carry):
        partial_stage(p)
        return carry

    lax.fori_loop(0, EARLY, partials, 0)

    stages = (
        (tower_stage, 0),
        (gather_stage, 4),
        (loss_stage, 8),
        (spread_stage, 12),
        (back_stage, 16),
        (rows_stage, LAST),
    )

    def tick(t, carry):
        for stage, lag in stages:

            @pl.when((t >= lag) & (t < lag + CHUNKS))
            def _():
                stage(t - lag)

            if lag == 0:

                @pl.when((t < 2 * (PAIRS - EARLY)) & (lax.rem(t, 2) == 0))
                def _():
                    partial_stage(EARLY + lax.div(t, 2))

        return carry

    lax.fori_loop(0, LAST + CHUNKS, tick, 0)

    wait(score_in, score_sem.at[0])
    lane = lax.broadcasted_iota(jnp.int32, (8, 128), 1)
    packed = jnp.zeros((8, 128), jnp.float32)
    for i in range(OWN):
        packed = packed + jnp.where(lane == i, score_in[i], 0.0)
    scores_ref[...] = packed

    wait(pooled.at[pl.ds(0, N - 1)], send_sem.at[0])
    wait(part_out.at[pl.ds(CHUNKS - 2, 2)], part_send_sem.at[PAIRS - 1])
    wait(head_out.at[:, pl.ds(0, N - 1)], send_sem.at[2])
    wait(row_out.at[pl.ds(0, CHUNKS - 1)], send_sem.at[3])
    wait(line_grad.at[pl.ds(0, CHUNKS - 1)], send_sem.at[4])
    wait(full_grad.at[:, pl.ds(0, N - 1)], send_sem.at[5])
    wait(own_first_grad, send_sem.at[6])
    wait(table_grad.at[:, pl.ds(0, N - 1)], send_sem.at[7])
    for e in range(OWN):

        @pl.when(score_target(e) != group)
        def _():
            wait(score_out.at[e], score_send_sem.at[e])

    wait(table_grad, grad_sem.at[0])


def on_device(
    looked_rows,
    lengths,
    assign,
    labels,
    tower_first,
    bias_first,
    tower_second,
    bias_second,
    over_weight,
    over_bias,
    out_weight,
):
    batch = looked_rows.shape[1]
    block = batch // (2 * N)
    bf16, f32 = jnp.bfloat16, jnp.float32
    any_spec = pl.BlockSpec(memory_space=pl.ANY)
    vmem_spec = pl.BlockSpec(memory_space=pltpu.VMEM)
    dma = pltpu.SemaphoreType.DMA
    scores, grad = pl.pallas_call(
        kernel,
        name="tower_step",
        out_shape=(
            jax.ShapeDtypeStruct((8, 128), f32),
            jax.ShapeDtypeStruct((2, N, block, E), bf16),
        ),
        in_specs=[any_spec] * 11,
        out_specs=(vmem_spec, any_spec),
        scratch_shapes=[
            pltpu.SMEM(assign.shape, jnp.int32),
            pltpu.SMEM(labels.shape, jnp.int32),
            pltpu.VMEM(bias_first.shape, bf16),
            pltpu.VMEM(bias_second.shape, bf16),
            pltpu.VMEM((H // 128, 128), bf16),
            pltpu.VMEM((H // 128, 128), bf16),
            pltpu.VMEM((2 * batch, E), bf16),
            pltpu.VMEM((batch // UNIT, UNIT), jnp.int32),
            pltpu.VMEM((batch // UNIT, 2 * UNIT), f32),
            pltpu.VMEM((SLOTS, E, TW), bf16),
            pltpu.VMEM((TW, TW), bf16),
            pltpu.VMEM((TW, H), bf16),
            pltpu.SMEM((N,), jnp.int32),
            pltpu.VMEM((N, PAIRS, 2, WIDE, E), bf16),
            pltpu.VMEM((PAIRS, N, 2, WIDE, E), bf16),
            pltpu.VMEM((CHUNKS, ROWS, TW), bf16),
            pltpu.VMEM((CHUNKS, ROWS, TW), bf16),
            pltpu.VMEM((CHUNKS, ROWS, TW), f32),
            pltpu.VMEM((CHUNKS, ROWS, TW), f32),
            pltpu.VMEM((CHUNKS, N, 16, QUARTER), bf16),
            pltpu.VMEM((CHUNKS, N, 16, QUARTER), bf16),
            pltpu.VMEM((64, 128), f32),
            pltpu.VMEM((16, 128), f32),
            pltpu.VMEM((16, 128), f32),
            pltpu.VMEM((CHUNKS, SHARE, 16, 128), bf16),
            pltpu.VMEM((CHUNKS // 2, N, 16, 128), bf16),
            pltpu.VMEM((CHUNKS // 2, 16, 128), bf16),
            pltpu.VMEM((CHUNKS, SHARE, 16, 128), bf16),
            pltpu.VMEM((CHUNKS, 16, QUARTER), bf16),
            pltpu.VMEM((CHUNKS, N, 16, QUARTER), bf16),
            pltpu.VMEM((CHUNKS, ROWS, TW), bf16),
            pltpu.VMEM((CHUNKS, ROWS, TW), bf16),
            pltpu.VMEM((CHUNKS, N, 2, ROWS, E), bf16),
            pltpu.VMEM((OWN, 8, 128), f32),
            pltpu.VMEM((OWN, 8, 128), f32),
            dma((11,)),
            dma((8,)),
            dma((PAIRS,)),
            dma((CHUNKS,)),
            dma((CHUNKS,)),
            dma((CHUNKS // 2,)),
            dma((CHUNKS,)),
            dma((CHUNKS,)),
            dma((CHUNKS,)),
            dma((1,)),
            dma((1,)),
            dma((OWN,)),
            dma((PAIRS,)),
        ],
        compiler_params=pltpu.CompilerParams(
            collective_id=0, has_side_effects=True, vmem_limit_bytes=63 * 2**20
        ),
    )(
        looked_rows.reshape(2 * batch, E),
        lengths.reshape(batch // UNIT, UNIT),
        assign,
        labels,
        tower_first.reshape(SLOTS, E, TW),
        bias_first,
        tower_second[0],
        bias_second,
        over_weight,
        over_bias.reshape(H // 128, 128),
        out_weight.reshape(H // 128, 128),
    )
    return scores[0, :OWN], grad.reshape(1, batch, E)


def solution(mesh):
    return jax.shard_map(
        on_device,
        mesh=mesh,
        in_specs=(
            P(("group", "local"), None, None, None),
            P(("group", "local"), None),
            P("group", None),
            P("local"),
            P("group", None, None),
            P("group", None),
            P("group", None, None),
            P("group", None),
            P("group", None),
            P(),
            P(),
        ),
        out_specs=(P(("local", "group")), P(("group", "local"), None, None)),
        check_vma=False,
    )
```
